32 devices in a mesh: band: 16 (over z, y, x), mp: 2 (over core).
Axes of the slice: x: 2, y: 2, z: 4, core: 2. Of those that a mesh axis runs over, the one named last changes fastest.
Arguments:
- grid_nodes: bfloat16 [65536, 512], P('band', 'mp'), may hold values from -6 to 6
- mesh_nodes: bfloat16 [8192, 512], P('band', 'mp'), may hold values from -6 to 6
- send_weight: bfloat16 [512, 512], P(None, 'mp'), may hold values from -0.25 to 0.25
- self_weight: bfloat16 [512, 512], P(None, 'mp'), may hold values from -0.25 to 0.25
- pooled_weight: bfloat16 [512, 512], P(None, 'mp'), may hold values from -0.25 to 0.25
- out_weight: bfloat16 [512, 2, 512], P('mp'), may hold values from -0.25 to 0.25
- encode_source: int32 [3072], P('band'), may hold values from 0 to 31
- encode_slot: int32 [3072], P('band'), may hold values from 0 to 15
- encode_tiles: bfloat16 [3072, 128, 128], P('band'), may hold values from -0.078125 to 0.078125
- slot_block: int32 [16, 16], P('band'), may hold values from 0 to 3
- decode_slot: int32 [3072], P('band'), may hold values from 0 to 15
- decode_target: int32 [3072], P('band'), may hold values from 0 to 31
- decode_tiles: bfloat16 [3072, 128, 128], P('band'), may hold values from -0.21875 to 0.21875
Outputs:
- grid_state: bfloat16 [65536, 512], P('band', 'mp')
- mesh_state: bfloat16 [8192, 512], P('band', 'mp')
The draws below stay inside these ranges and needn't reach their ends.
All inputs are finite; a program needn't handle non-finite values.
Results may differ from the reference program's by a relative error of at most 0.005.
Values may be sent and summed in bfloat16 or wider, within the bound.
A program may use at most 192 MiB of HBM per device.

```python
import math
import jax
import jax.numpy as jnp
import numpy as np
from jax import lax

D = 512
HID = 512
BLOCK = 128
GB_DEV = 32
MB_DEV = 4
TPB = 6
E_ALL = 3072
GRID = 65536
MESH = 8192
N_BAND = 16


def plant(values, rng, least, largest):
    longest = values.shape.index(max(values.shape))
    spots = []
    for shift in (0, 1):
        where = [jax.random.randint(jax.random.fold_in(rng, axis), (), 0, length) for axis, length in enumerate(values.shape)]
        where[longest] = (where[longest] + shift) % values.shape[longest]
        spots.append(tuple(where))
    return values.at[spots[0]].set(least).at[spots[1]].set(largest)


def block_levels(rng, shape, cuts, least, top_value):
    gain, own = 1.0, jax.random.fold_in(rng, 6)
    for axis_at, blocks in cuts:
        heights = jnp.exp(jax.random.uniform(jax.random.fold_in(own, axis_at), (blocks,), jnp.float32, least / len(cuts), top_value / len(cuts)))
        gain = gain * jnp.repeat(heights, shape[axis_at] // blocks).reshape([-1 if axis == axis_at else 1 for axis in range(len(shape))])
    return gain


def cumulative_ranks(amount, slope):
    loads = [(1 << 20) // math.isqrt(rank ** slope) + 1 for rank in range(1, amount + 1)]
    deviation = 1 + sum(loads) // (1 << 30)
    return np.cumsum(np.array([max(1, weight // deviation) for weight in loads]))


def ranked_ids(stream_key, extent, amount, skew):
    grid = cumulative_ranks(amount, skew)
    ticket = jax.random.randint(jax.random.fold_in(stream_key, 1), extent, 0, int(grid[amount - 1]))
    standing = jnp.searchsorted(jnp.asarray(grid, jnp.int32), ticket, side="right")
    return jax.random.permutation(jax.random.fold_in(stream_key, 2), amount)[standing].astype(jnp.int32)


def bell_draw(key, extent, width, most, cuts=(), held_as=jnp.bfloat16):
    values = jax.random.normal(key, extent, jnp.float32) * width
    if len(cuts) > 0:
        values = block_levels(key, extent, cuts, -0.22, 0.18) * values
    return jnp.clip(values, min=-most, max=most).astype(held_as)


def setup_inputs(seed: int = 0) -> dict:
    seeds = jax.random.split(jax.random.key(seed), 14)
    return {
        "grid_nodes": bell_draw(seeds[0], (GRID, D), 1.0, 6.0, ((0, 16), (1, 2))),
        "mesh_nodes": bell_draw(seeds[1], (MESH, D), 1.0, 6.0, ((0, 16), (1, 2))),
        "send_weight": bell_draw(seeds[2], (D, D), D ** -0.5, 0.25, ((1, 2),)),
        "self_weight": bell_draw(seeds[3], (D, HID), D ** -0.5, 0.25, ((1, 2),)),
        "pooled_weight": bell_draw(seeds[4], (D, HID), D ** -0.5, 0.25, ((1, 2),)),
        "out_weight": bell_draw(seeds[5], (HID, 2, D), HID ** -0.5, 0.25, ((0, 2),)),
        "encode_source": plant(jax.random.randint(seeds[6], (E_ALL,), 0, GB_DEV), jax.random.fold_in(seeds[6], 1), 0, GB_DEV - 1).astype(jnp.int32),
        "encode_slot": plant(ranked_ids(seeds[7], (E_ALL,), N_BAND, 2), jax.random.fold_in(seeds[7], 3), 0, N_BAND - 1).astype(jnp.int32),
        "encode_tiles": bell_draw(seeds[8], (E_ALL, BLOCK, BLOCK), (TPB * GB_DEV * BLOCK // MB_DEV) ** -0.5, 0.078125, ((0, 16),)),
        "slot_block": plant(jax.random.randint(seeds[9], (N_BAND, N_BAND), 0, MB_DEV), jax.random.fold_in(seeds[9], 1), 0, MB_DEV - 1).astype(jnp.int32),
        "decode_slot": plant(ranked_ids(seeds[10], (E_ALL,), N_BAND, 2), jax.random.fold_in(seeds[10], 3), 0, N_BAND - 1).astype(jnp.int32),
        "decode_target": plant(jax.random.randint(seeds[11], (E_ALL,), 0, GB_DEV), jax.random.fold_in(seeds[11], 1), 0, GB_DEV - 1).astype(jnp.int32),
        "decode_tiles": bell_draw(seeds[12], (E_ALL, BLOCK, BLOCK), (TPB * BLOCK) ** -0.5, 0.21875, ((0, 16),)),
    }


def reference(grid_nodes, mesh_nodes, send_weight, self_weight, pooled_weight, out_weight, encode_source, encode_slot, encode_tiles, slot_block, decode_slot, decode_target, decode_tiles):
    tile_count = TPB * GB_DEV
    message = jax.nn.silu(jnp.dot(grid_nodes, send_weight, preferred_element_type=jnp.float32)).astype(jnp.bfloat16)
    message_blocks = message.reshape(N_BAND, GB_DEV, BLOCK, D)
    source_rows = encode_source.reshape(N_BAND, tile_count)
    slot_rows = encode_slot.reshape(N_BAND, tile_count)
    tile_rows = encode_tiles.reshape(N_BAND, tile_count, BLOCK, BLOCK)

    def encode_band(aggregate, inputs):
        band_blocks, sources, slots, tiles, linked = inputs
        picked = band_blocks[sources]
        partial_value = jnp.einsum("eij,ejc->eic", tiles.astype(jnp.float32), picked.astype(jnp.float32))
        slot_sum = jax.ops.segment_sum(partial_value, slots, num_segments=N_BAND)
        targets = jnp.arange(N_BAND, dtype=jnp.int32) * MB_DEV + linked
        return aggregate.at[targets].add(slot_sum), None

    start = jnp.zeros((N_BAND * MB_DEV, BLOCK, D), jnp.float32)
    aggregate, _ = lax.scan(encode_band, start, (message_blocks, source_rows, slot_rows, tile_rows, slot_block))
    pooled = aggregate.reshape(N_BAND * MB_DEV * BLOCK, D).astype(jnp.bfloat16)
    inner = jnp.dot(mesh_nodes, self_weight, preferred_element_type=jnp.float32) + jnp.dot(pooled, pooled_weight, preferred_element_type=jnp.float32)
    hidden = jax.nn.silu(inner).astype(jnp.bfloat16)
    projected = jnp.dot(hidden, out_weight.reshape(HID, 2 * D), preferred_element_type=jnp.float32).reshape(-1, 2, D)
    mesh_state = (mesh_nodes.astype(jnp.float32) + projected[:, 0, :]).astype(jnp.bfloat16)
    decode_source = projected[:, 1, :].astype(jnp.bfloat16).reshape(N_BAND * MB_DEV, BLOCK, D)

    def decode_band(inputs):
        slots, targets, tiles, linked, grid_band = inputs
        mesh_index = slots * MB_DEV + linked[slots]
        picked = decode_source[mesh_index]
        partial_value = jnp.einsum("eij,ejc->eic", tiles.astype(jnp.float32), picked.astype(jnp.float32))
        grid_sum = jax.ops.segment_sum(partial_value, targets, num_segments=GB_DEV)
        return (grid_band.astype(jnp.float32) + grid_sum.reshape(GB_DEV * BLOCK, D)).astype(jnp.bfloat16)

    grid_state = lax.map(decode_band, (decode_slot.reshape(N_BAND, tile_count), decode_target.reshape(N_BAND, tile_count), decode_tiles.reshape(N_BAND, tile_count, BLOCK, BLOCK), slot_block, grid_nodes.reshape(N_BAND, GB_DEV * BLOCK, D)))
    return grid_state.reshape(N_BAND * GB_DEV * BLOCK, D), mesh_state
```

```python
import functools

import jax
import jax.numpy as jnp
from jax import lax
from jax.experimental import pallas as pl
from jax.experimental.pallas import tpu as pltpu
from jax.sharding import PartitionSpec as P

VMEM = pltpu.VMEM
VMEM_LIMIT = 56 * 1024 * 1024


def divisor_at_most(count, most):
    return max(part for part in range(1, most + 1) if count % part == 0)


def tile_sums(group, tile_at, rows_ref, tiles_ref, into_ref, from_ref, total):
    for local in range(group):
        place = tile_at + local
        product = jnp.dot(
            tiles_ref[local], rows_ref[from_ref[place]], preferred_element_type=jnp.float32
        )
        total[into_ref[place]] += product


def encode_kernel(group, source_ref, slot_ref, message_ref, tiles_ref, out_ref, total):
    step = pl.program_id(0)

    @pl.when(step == 0)
    def _():
        total[...] = jnp.zeros_like(total)

    tile_sums(group, step * group, message_ref, tiles_ref, slot_ref, source_ref, total)

    @pl.when(step == pl.num_programs(0) - 1)
    def _():
        out_ref[...] = total[...].astype(out_ref.dtype)


def decode_kernel(group, slot_ref, target_ref, grid_ref, rows_ref, tiles_ref, out_ref, total):
    step = pl.program_id(0)

    @pl.when(step == 0)
    def _():
        total[...] = grid_ref[...].astype(jnp.float32)

    tile_sums(group, step * group, rows_ref, tiles_ref, target_ref, slot_ref, total)

    @pl.when(step == pl.num_programs(0) - 1)
    def _():
        out_ref[...] = total[...].astype(out_ref.dtype)


def whole(array):
    return pl.BlockSpec(array.shape, lambda step, *_: (0,) * array.ndim)


def encode(message_blocks, tiles, source, slot, slots):
    count, edge, _ = tiles.shape
    width = message_blocks.shape[2]
    group = divisor_at_most(count, 24)
    out = jax.ShapeDtypeStruct((slots, edge, width), jnp.bfloat16)
    return pl.pallas_call(
        functools.partial(encode_kernel, group),
        out_shape=out,
        grid_spec=pltpu.PrefetchScalarGridSpec(
            num_scalar_prefetch=2,
            grid=(count // group,),
            in_specs=[
                whole(message_blocks),
                pl.BlockSpec((group, edge, edge), lambda step, *_: (step, 0, 0)),
            ],
            out_specs=whole(out),
            scratch_shapes=[VMEM((slots, edge, width), jnp.float32)],
        ),
        compiler_params=pltpu.CompilerParams(vmem_limit_bytes=VMEM_LIMIT),
        name="encode",
    )(source, slot, message_blocks, tiles)


def decode(grid_blocks, rows, tiles, slot, target):
    count, edge, _ = tiles.shape
    group = divisor_at_most(count, 24)
    return pl.pallas_call(
        functools.partial(decode_kernel, group),
        out_shape=jax.ShapeDtypeStruct(grid_blocks.shape, jnp.bfloat16),
        grid_spec=pltpu.PrefetchScalarGridSpec(
            num_scalar_prefetch=2,
            grid=(count // group,),
            in_specs=[
                whole(grid_blocks),
                whole(rows),
                pl.BlockSpec((group, edge, edge), lambda step, *_: (step, 0, 0)),
            ],
            out_specs=whole(grid_blocks),
            scratch_shapes=[VMEM(grid_blocks.shape, jnp.float32)],
        ),
        compiler_params=pltpu.CompilerParams(vmem_limit_bytes=VMEM_LIMIT),
        name="decode",
    )(slot, target, grid_blocks, rows, tiles)


def per_device(
    grid_nodes,
    mesh_nodes,
    send_weight,
    self_weight,
    pooled_weight,
    out_weight,
    encode_source,
    encode_slot,
    encode_tiles,
    slot_block,
    decode_slot,
    decode_target,
    decode_tiles,
):
    band_count = lax.axis_size("band")
    tile_edge = encode_tiles.shape[1]
    feature_width = grid_nodes.shape[1]
    grid_blocks = grid_nodes.shape[0] // tile_edge
    mesh_blocks = mesh_nodes.shape[0] // tile_edge
    full_grid = lax.all_gather(grid_nodes, "mp", axis=1, tiled=True)
    message = jax.nn.silu(
        jnp.dot(full_grid, send_weight, preferred_element_type=jnp.float32)
    ).astype(jnp.bfloat16)
    message_blocks = message.reshape(grid_blocks, tile_edge, feature_width)
    slot_sums = encode(message_blocks, encode_tiles, encode_source, encode_slot, band_count)
    arrived, owner_block = (
        lax.all_to_all(slot_sums, "band", split_axis=0, concat_axis=0, tiled=True),
        lax.all_to_all(slot_block[0], "band", split_axis=0, concat_axis=0, tiled=True),
    )
    selector = (owner_block[None, :] == jnp.arange(mesh_blocks, dtype=jnp.int32)[:, None]).astype(
        jnp.float32
    )
    aggregate = jnp.einsum("bs,sic->bic", selector, arrived.astype(jnp.float32), precision=lax.Precision.HIGHEST)
    pooled = aggregate.reshape(-1, feature_width).astype(jnp.bfloat16)
    mesh_full, pooled_full = (
        lax.all_gather(mesh_nodes, "mp", axis=1, tiled=True),
        lax.all_gather(pooled, "mp", axis=1, tiled=True),
    )
    inner_sum = jnp.dot(mesh_full, self_weight, preferred_element_type=jnp.float32) + jnp.dot(
        pooled_full, pooled_weight, preferred_element_type=jnp.float32
    )
    hidden = jax.nn.silu(inner_sum).astype(jnp.bfloat16)
    partial_out = jnp.dot(
        hidden, out_weight.reshape(hidden.shape[1], -1), preferred_element_type=jnp.float32
    )
    partial_out = partial_out.reshape(hidden.shape[0], 2, -1)
    reduced = lax.psum_scatter(partial_out, "mp", scatter_dimension=2, tiled=True)
    mesh_state = (mesh_nodes.astype(jnp.float32) + reduced[:, 0, :]).astype(jnp.bfloat16)
    decode_source = (
        reduced[:, 1, :].astype(jnp.bfloat16).reshape(mesh_blocks, tile_edge, feature_width)
    )
    outgoing = sum(
        jnp.where(owner_block[:, None, None] == block, decode_source[block], 0)
        for block in range(mesh_blocks)
    )
    returned = lax.all_to_all(outgoing, "band", split_axis=0, concat_axis=0, tiled=True)
    grid_state = decode(
        grid_nodes.reshape(grid_blocks, tile_edge, feature_width),
        returned,
        decode_tiles,
        decode_slot,
        decode_target,
    ).reshape(grid_nodes.shape)
    return (grid_state, mesh_state)


def solution(mesh):
    return jax.shard_map(
        per_device,
        mesh=mesh,
        in_specs=(
            P("band", "mp"),
            P("band", "mp"),
            P(None, "mp"),
            P(None, "mp"),
            P(None, "mp"),
            P("mp", None, None),
            P("band"),
            P("band"),
            P("band", None, None),
            P("band", None),
            P("band"),
            P("band"),
            P("band", None, None),
        ),
        out_specs=(P("band", "mp"), P("band", "mp")),
        check_vma=False,
    )
```

```python
import functools

import jax
import jax.numpy as jnp
from jax import lax
from jax.experimental import pallas as pl
from jax.experimental.pallas import tpu as pltpu
from jax.sharding import PartitionSpec as P

VMEM = pltpu.VMEM
VMEM_LIMIT = 56 * 1024 * 1024


def divisor_at_most(count, most):
    return max(part for part in range(1, most + 1) if count % part == 0)


def tile_sums(group, tile_at, rows_ref, tiles_ref, into_ref, from_ref, total):
    for local in range(group):
        place = tile_at + local
        product = jnp.dot(
            tiles_ref[local], rows_ref[from_ref[place]], preferred_element_type=jnp.float32
        )
        total[into_ref[place]] += product


def encode_kernel(group, source_ref, slot_ref, message_ref, tiles_ref, out_ref, total):
    step = pl.program_id(0)

    @pl.when(step == 0)
    def _():
        total[...] = jnp.zeros_like(total)

    tile_sums(group, step * group, message_ref, tiles_ref, slot_ref, source_ref, total)

    @pl.when(step == pl.num_programs(0) - 1)
    def _():
        out_ref[...] = total[...].astype(out_ref.dtype)


def decode_kernel(group, slot_ref, target_ref, grid_ref, rows_ref, tiles_ref, out_ref, total):
    step = pl.program_id(0)

    @pl.when(step == 0)
    def _():
        total[...] = grid_ref[...].astype(jnp.float32)

    tile_sums(group, step * group, rows_ref, tiles_ref, target_ref, slot_ref, total)

    @pl.when(step == pl.num_programs(0) - 1)
    def _():
        out_ref[...] = total[...].astype(out_ref.dtype)


def whole(array):
    return pl.BlockSpec(array.shape, lambda step, *_: (0,) * array.ndim)


def encode(message_blocks, tiles, source, slot, slots):
    count, edge, _ = tiles.shape
    width = message_blocks.shape[2]
    group = divisor_at_most(count, 24)
    out = jax.ShapeDtypeStruct((slots, edge, width), jnp.bfloat16)
    return pl.pallas_call(
        functools.partial(encode_kernel, group),
        out_shape=out,
        grid_spec=pltpu.PrefetchScalarGridSpec(
            num_scalar_prefetch=2,
            grid=(count // group,),
            in_specs=[
                whole(message_blocks),
                pl.BlockSpec((group, edge, edge), lambda step, *_: (step, 0, 0)),
            ],
            out_specs=whole(out),
            scratch_shapes=[VMEM((slots, edge, width), jnp.float32)],
        ),
        compiler_params=pltpu.CompilerParams(vmem_limit_bytes=VMEM_LIMIT),
        name="encode",
    )(source, slot, message_blocks, tiles)


def decode(grid_blocks, rows, tiles, slot, target):
    count, edge, _ = tiles.shape
    group = divisor_at_most(count, 24)
    return pl.pallas_call(
        functools.partial(decode_kernel, group),
        out_shape=jax.ShapeDtypeStruct(grid_blocks.shape, jnp.bfloat16),
        grid_spec=pltpu.PrefetchScalarGridSpec(
            num_scalar_prefetch=2,
            grid=(count // group,),
            in_specs=[
                whole(grid_blocks),
                whole(rows),
                pl.BlockSpec((group, edge, edge), lambda step, *_: (step, 0, 0)),
            ],
            out_specs=whole(grid_blocks),
            scratch_shapes=[VMEM(grid_blocks.shape, jnp.float32)],
        ),
        compiler_params=pltpu.CompilerParams(vmem_limit_bytes=VMEM_LIMIT),
        name="decode",
    )(slot, target, grid_blocks, rows, tiles)


def silu(value):
    return value / (1.0 + jnp.exp(-value))


def push(source, target, send_sem, recv_sem, device):
    return pltpu.make_async_remote_copy(
        src_ref=source,
        dst_ref=target,
        send_sem=send_sem,
        recv_sem=recv_sem,
        device_id=device,
        device_id_type=pl.DeviceIdType.MESH,
    )


def matmul(left, right):
    return jnp.dot(left, right, preferred_element_type=jnp.float32)


def message_kernel(parts, grid_hbm, weight_ref, out_ref, own, other, load_sem, send_sem, recv_sem):
    me = lax.axis_index("mp")
    peer = 1 - me
    rows = own.shape[0] // parts
    half = own.shape[1]

    def part(ref, at):
        return ref.at[pl.ds(at * rows, rows)]

    loads = [
        pltpu.make_async_copy(part(grid_hbm, at), part(own, at), load_sem.at[at])
        for at in range(parts)
    ]
    for load in loads:
        load.start()
    barrier = pltpu.get_barrier_semaphore()
    pl.semaphore_signal(
        barrier, inc=1, device_id={"mp": peer}, device_id_type=pl.DeviceIdType.MESH
    )
    pl.semaphore_wait(barrier, 1)
    sends = [
        push(part(grid_hbm, at), part(other, at), send_sem.at[at], recv_sem.at[at], {"mp": peer})
        for at in range(parts)
    ]
    for send in sends:
        send.start()
    own_weight = weight_ref[pl.ds(pl.multiple_of(me * half, half), half), :]
    other_weight = weight_ref[pl.ds(pl.multiple_of(peer * half, half), half), :]
    for at in range(parts):
        loads[at].wait()
        sends[at].wait_recv()
        span = pl.ds(at * rows, rows)
        total = matmul(own[span, :], own_weight) + matmul(other[span, :], other_weight)
        out_ref[span, :] = silu(total).astype(out_ref.dtype)
    for send in sends:
        send.wait_send()


def messages(grid_nodes, send_weight):
    rows, half = grid_nodes.shape
    parts = 8
    return pl.pallas_call(
        functools.partial(message_kernel, parts),
        out_shape=jax.ShapeDtypeStruct((rows, send_weight.shape[1]), jnp.bfloat16),
        in_specs=[pl.BlockSpec(memory_space=pl.ANY), pl.BlockSpec(memory_space=VMEM)],
        out_specs=pl.BlockSpec(memory_space=VMEM),
        scratch_shapes=[VMEM((rows, half), jnp.bfloat16)] * 2
        + [pltpu.SemaphoreType.DMA((parts,))] * 3,
        compiler_params=pltpu.CompilerParams(
            collective_id=0, has_side_effects=True, vmem_limit_bytes=VMEM_LIMIT
        ),
        name="messages",
    )(grid_nodes, send_weight)


def node_kernel(
    sums_ref, linked_ref, mesh_ref, self_ref, pooled_weight_ref, out_weight_ref,
    state_ref, returned_ref,
    link_out, link_in, arrived, mesh_other, weight_other, pooled, pooled_other,
    hidden, hidden_other, inner, total, projected, stage,
    link_send, link_recv, sum_send, sum_recv, back_send, back_recv, mp_send, mp_recv,
):
    bands = sums_ref.shape[0]
    blocks, edge, half = total.shape
    width = self_ref.shape[1] * 2
    me = lax.axis_index("band")
    core = lax.axis_index("mp")
    peer = 1 - core
    across = {"mp": peer}
    mine = pl.multiple_of(core * half, half)
    theirs = pl.multiple_of(peer * half, half)

    barrier = pltpu.get_barrier_semaphore()

    def greet(hop, carry):
        pl.semaphore_signal(
            barrier,
            inc=1,
            device_id={"band": lax.rem(me + hop, bands)},
            device_id_type=pl.DeviceIdType.MESH,
        )
        return carry

    lax.fori_loop(1, bands, greet, 0)
    pl.semaphore_signal(barrier, inc=1, device_id=across, device_id_type=pl.DeviceIdType.MESH)

    def spread(patch, carry):
        link_out[patch] = jnp.full(link_out.shape[1:], linked_ref[0, patch], jnp.int32)
        return carry

    lax.fori_loop(0, bands, spread, 0)
    pl.semaphore_wait(barrier, bands)

    def link_copy(patch):
        return push(
            link_out.at[patch], link_in.at[me], link_send.at[patch], link_recv.at[me],
            {"band": patch},
        )

    def sum_copy(patch):
        return push(
            sums_ref.at[patch], arrived.at[me], sum_send.at[patch], sum_recv.at[me],
            {"band": patch},
        )

    def back_copy(band):
        return push(
            stage.at[band], returned_ref.at[me], back_send.at[band], back_recv.at[me],
            {"band": band},
        )

    def send_links(hop, carry):
        link_copy(lax.rem(me + hop, bands)).start()
        return carry

    def send_sums(hop, carry):
        sum_copy(lax.rem(me + hop, bands)).start()
        return carry

    lax.fori_loop(1, bands, send_links, 0)
    lax.fori_loop(1, bands, send_sums, 0)

    mesh_copy = push(mesh_ref, mesh_other, mp_send.at[0], mp_recv.at[0], across)
    mesh_copy.start()
    weight_copies = [
        push(
            out_weight_ref.at[:, pl.ds(pl.multiple_of(which * width + theirs, half), half)],
            weight_other.at[which],
            mp_send.at[1 + which],
            mp_recv.at[1 + which],
            across,
        )
        for which in range(2)
    ]
    for copy in weight_copies:
        copy.start()

    inner[...] = matmul(mesh_ref[...], self_ref[pl.ds(mine, half), :])
    mesh_copy.wait()
    inner[...] += matmul(mesh_other[...], self_ref[pl.ds(theirs, half), :])

    own = sums_ref[me].astype(jnp.float32)
    own_link = link_out[me, 0:1, :]
    for block in range(blocks):
        total[block] = jnp.where(own_link == block, own, 0.0)

    def gather(hop, carry):
        band = lax.rem(me + bands - hop, bands)
        push(
            link_out.at[band], link_in.at[band], link_send.at[band], link_recv.at[band],
            {"band": band},
        ).wait_recv()
        push(
            sums_ref.at[band], arrived.at[band], sum_send.at[band], sum_recv.at[band],
            {"band": band},
        ).wait_recv()
        value = arrived[band].astype(jnp.float32)
        link = link_in[band, 0:1, :]
        for block in range(blocks):
            total[block] += jnp.where(link == block, value, 0.0)
        return carry

    lax.fori_loop(1, bands, gather, 0)

    pooled[...] = total[...].reshape(pooled.shape).astype(pooled.dtype)
    pooled_copy = push(pooled, pooled_other, mp_send.at[3], mp_recv.at[3], across)
    pooled_copy.start()
    inner[...] += matmul(pooled[...], pooled_weight_ref[pl.ds(mine, half), :])
    pooled_copy.wait()
    inner[...] += matmul(pooled_other[...], pooled_weight_ref[pl.ds(theirs, half), :])
    hidden[...] = silu(inner[...]).astype(hidden.dtype)
    hidden_copy = push(hidden, hidden_other, mp_send.at[4], mp_recv.at[4], across)
    hidden_copy.start()
    for which in range(2):
        columns = pl.ds(pl.multiple_of(which * width + mine, half), half)
        projected[which] = matmul(hidden[...], out_weight_ref[:, columns])
    for copy in weight_copies:
        copy.wait()
    hidden_copy.wait()
    source = projected[1] + matmul(hidden_other[...], weight_other[1])
    total[...] = source.astype(jnp.bfloat16).astype(jnp.float32).reshape(total.shape)

    def picked(link):
        value = total[0]
        for block in range(1, blocks):
            value = jnp.where(link == block, total[block], value)
        return value.astype(stage.dtype)

    def send_back(hop, carry):
        band = lax.rem(me + hop, bands)
        stage[band] = picked(link_in[band, 0:1, :])
        back_copy(band).start()
        return carry

    lax.fori_loop(1, bands, send_back, 0)
    returned_ref[me] = picked(own_link)
    residual = projected[0] + matmul(hidden_other[...], weight_other[0])
    state_ref[...] = (mesh_ref[...].astype(jnp.float32) + residual).astype(state_ref.dtype)

    def finish(hop, carry):
        band = lax.rem(me + bands - hop, bands)
        push(
            stage.at[band], returned_ref.at[band], back_send.at[band], back_recv.at[band],
            {"band": band},
        ).wait_recv()
        link_copy(band).wait_send()
        sum_copy(band).wait_send()
        back_copy(band).wait_send()
        return carry

    lax.fori_loop(1, bands, finish, 0)


def update_nodes(sums, linked, mesh_nodes, self_weight, pooled_weight, out_weight):
    bands, edge, half = sums.shape
    rows = mesh_nodes.shape[0]
    flat_weight = out_weight.reshape(out_weight.shape[0], -1)
    nodes = VMEM((rows, half), jnp.bfloat16)
    by_band = pltpu.SemaphoreType.DMA((bands,))
    by_use = pltpu.SemaphoreType.DMA((5,))
    vmem = pl.BlockSpec(memory_space=VMEM)
    return pl.pallas_call(
        node_kernel,
        out_shape=(
            jax.ShapeDtypeStruct(mesh_nodes.shape, jnp.bfloat16),
            jax.ShapeDtypeStruct(sums.shape, jnp.bfloat16),
        ),
        in_specs=[vmem, pl.BlockSpec(memory_space=pltpu.SMEM)] + [vmem] * 4,
        out_specs=(vmem, vmem),
        scratch_shapes=[
            VMEM((bands, 8, half), jnp.int32),
            VMEM((bands, 8, half), jnp.int32),
            VMEM(sums.shape, jnp.bfloat16),
            nodes,
            VMEM((2, out_weight.shape[0], half), jnp.bfloat16),
            nodes,
            nodes,
            nodes,
            nodes,
            VMEM((rows, half), jnp.float32),
            VMEM((rows // edge, edge, half), jnp.float32),
            VMEM((2, rows, half), jnp.float32),
            VMEM(sums.shape, jnp.bfloat16),
        ]
        + [by_band] * 6
        + [by_use] * 2,
        compiler_params=pltpu.CompilerParams(
            collective_id=1, has_side_effects=True, vmem_limit_bytes=VMEM_LIMIT
        ),
        name="update_nodes",
    )(sums, linked, mesh_nodes, self_weight, pooled_weight, flat_weight)


def per_device(
    grid_nodes,
    mesh_nodes,
    send_weight,
    self_weight,
    pooled_weight,
    out_weight,
    encode_source,
    encode_slot,
    encode_tiles,
    slot_block,
    decode_slot,
    decode_target,
    decode_tiles,
):
    band_count = lax.axis_size("band")
    tile_edge = encode_tiles.shape[1]
    feature_width = grid_nodes.shape[1]
    grid_blocks = grid_nodes.shape[0] // tile_edge
    message = messages(grid_nodes, send_weight)
    message_blocks = message.reshape(grid_blocks, tile_edge, feature_width)
    slot_sums = encode(message_blocks, encode_tiles, encode_source, encode_slot, band_count)
    mesh_state, returned = update_nodes(
        slot_sums, slot_block, mesh_nodes, self_weight, pooled_weight, out_weight
    )
    grid_state = decode(
        grid_nodes.reshape(grid_blocks, tile_edge, feature_width),
        returned,
        decode_tiles,
        decode_slot,
        decode_target,
    ).reshape(grid_nodes.shape)
    return (grid_state, mesh_state)


def solution(mesh):
    return jax.shard_map(
        per_device,
        mesh=mesh,
        in_specs=(
            P("band", "mp"),
            P("band", "mp"),
            P(None, "mp"),
            P(None, "mp"),
            P(None, "mp"),
            P("mp", None, None),
            P("band"),
            P("band"),
            P("band", None, None),
            P("band", None),
            P("band"),
            P("band"),
            P("band", None, None),
        ),
        out_specs=(P("band", "mp"), P("band", "mp")),
        check_vma=False,
    )
```

```python
import functools

import jax
import jax.numpy as jnp
from jax import lax
from jax.experimental import pallas as pl
from jax.experimental.pallas import tpu as pltpu
from jax.sharding import PartitionSpec as P

VMEM = pltpu.VMEM
VMEM_LIMIT = 56 * 1024 * 1024


def divisor_at_most(count, most):
    return max(part for part in range(1, most + 1) if count % part == 0)


def tile_sums(group, tile_at, rows_ref, tiles_ref, into_ref, from_ref, totals):
    for local in range(group):
        place = tile_at + local
        product = jnp.dot(
            tiles_ref[local], rows_ref[from_ref[place]], preferred_element_type=jnp.float32
        )
        totals[local % len(totals)][into_ref[place]] += product


def encode_kernel(group, source_ref, slot_ref, message_ref, tiles_ref, out_ref, *totals):
    step = pl.program_id(0)

    @pl.when(step == 0)
    def _():
        for total in totals:
            total[...] = jnp.zeros_like(total)

    tile_sums(group, step * group, message_ref, tiles_ref, slot_ref, source_ref, totals)

    @pl.when(step == pl.num_programs(0) - 1)
    def _():
        out_ref[...] = sum(total[...] for total in totals).astype(out_ref.dtype)


def decode_kernel(
    group, slot_ref, target_ref, grid_hbm, rows_ref, tiles_ref, out_ref, grid_ref, load_sem, *totals
):
    step = pl.program_id(0)
    load = pltpu.make_async_copy(grid_hbm, grid_ref, load_sem)

    @pl.when(step == 0)
    def _():
        load.start()
        for total in totals:
            total[...] = jnp.zeros_like(total)

    tile_sums(group, step * group, rows_ref, tiles_ref, target_ref, slot_ref, totals)

    @pl.when(step == pl.num_programs(0) - 1)
    def _():
        load.wait()
        summed = sum(total[...] for total in totals)
        out_ref[...] = (grid_ref[...].astype(jnp.float32) + summed).astype(out_ref.dtype)


def whole(array):
    return pl.BlockSpec(array.shape, lambda step, *_: (0,) * array.ndim)


def encode(message_blocks, tiles, source, slot, slots):
    count, edge, _ = tiles.shape
    width = message_blocks.shape[2]
    group = divisor_at_most(count, 48)
    out = jax.ShapeDtypeStruct((slots, edge, width), jnp.bfloat16)
    return pl.pallas_call(
        functools.partial(encode_kernel, group),
        out_shape=out,
        grid_spec=pltpu.PrefetchScalarGridSpec(
            num_scalar_prefetch=2,
            grid=(count // group,),
            in_specs=[
                whole(message_blocks),
                pl.BlockSpec((group, edge, edge), lambda step, *_: (step, 0, 0)),
            ],
            out_specs=whole(out),
            scratch_shapes=[VMEM((slots, edge, width), jnp.float32)] * 1,
        ),
        compiler_params=pltpu.CompilerParams(vmem_limit_bytes=VMEM_LIMIT),
        name="encode",
    )(source, slot, message_blocks, tiles)


def decode(grid_blocks, rows, tiles, slot, target):
    count, edge, _ = tiles.shape
    group = divisor_at_most(count, 48)
    return pl.pallas_call(
        functools.partial(decode_kernel, group),
        out_shape=jax.ShapeDtypeStruct(grid_blocks.shape, jnp.bfloat16),
        grid_spec=pltpu.PrefetchScalarGridSpec(
            num_scalar_prefetch=2,
            grid=(count // group,),
            in_specs=[
                pl.BlockSpec(memory_space=pl.ANY),
                whole(rows),
                pl.BlockSpec((group, edge, edge), lambda step, *_: (step, 0, 0)),
            ],
            out_specs=whole(grid_blocks),
            scratch_shapes=[VMEM(grid_blocks.shape, jnp.bfloat16), pltpu.SemaphoreType.DMA]
            + [VMEM(grid_blocks.shape, jnp.float32)] * 1,
        ),
        compiler_params=pltpu.CompilerParams(vmem_limit_bytes=VMEM_LIMIT),
        name="decode",
    )(slot, target, grid_blocks, rows, tiles)


def silu(value):
    return value / (1.0 + jnp.exp(-value))


def push(source, target, send_sem, recv_sem, device):
    return pltpu.make_async_remote_copy(
        src_ref=source,
        dst_ref=target,
        send_sem=send_sem,
        recv_sem=recv_sem,
        device_id=device,
        device_id_type=pl.DeviceIdType.MESH,
    )


def matmul(left, right):
    return jnp.dot(left, right, preferred_element_type=jnp.float32)


def message_kernel(parts, grid_hbm, weight_ref, out_ref, own, other, load_sem, send_sem, recv_sem):
    me = lax.axis_index("mp")
    peer = 1 - me
    rows = own.shape[0] // parts
    half = own.shape[1]

    def part(ref, at):
        return ref.at[pl.ds(at * rows, rows)]

    loads = [
        pltpu.make_async_copy(part(grid_hbm, at), part(own, at), load_sem.at[at])
        for at in range(parts)
    ]
    for load in loads:
        load.start()
    barrier = pltpu.get_barrier_semaphore()
    pl.semaphore_signal(
        barrier, inc=1, device_id={"mp": peer}, device_id_type=pl.DeviceIdType.MESH
    )
    pl.semaphore_wait(barrier, 1)
    sends = [
        push(part(grid_hbm, at), part(other, at), send_sem.at[at], recv_sem.at[at], {"mp": peer})
        for at in range(parts)
    ]
    for send in sends:
        send.start()
    own_weight = weight_ref[pl.ds(pl.multiple_of(me * half, half), half), :]
    other_weight = weight_ref[pl.ds(pl.multiple_of(peer * half, half), half), :]
    for at in range(parts):
        loads[at].wait()
        sends[at].wait_recv()
        span = pl.ds(at * rows, rows)
        total = matmul(own[span, :], own_weight) + matmul(other[span, :], other_weight)
        out_ref[span, :] = silu(total).astype(out_ref.dtype)
    for send in sends:
        send.wait_send()


def messages(grid_nodes, send_weight):
    rows, half = grid_nodes.shape
    parts = 8
    return pl.pallas_call(
        functools.partial(message_kernel, parts),
        out_shape=jax.ShapeDtypeStruct((rows, send_weight.shape[1]), jnp.bfloat16),
        in_specs=[pl.BlockSpec(memory_space=pl.ANY), pl.BlockSpec(memory_space=VMEM)],
        out_specs=pl.BlockSpec(memory_space=VMEM),
        scratch_shapes=[VMEM((rows, half), jnp.bfloat16)] * 2
        + [pltpu.SemaphoreType.DMA((parts,))] * 3,
        compiler_params=pltpu.CompilerParams(
            collective_id=0, has_side_effects=True, vmem_limit_bytes=VMEM_LIMIT
        ),
        name="messages",
    )(grid_nodes, send_weight)


def node_kernel(
    chunks, sums_ref, linked_ref, mesh_ref, self_ref, pooled_weight_ref, out_weight_ref,
    state_ref, returned_ref,
    link_out, link_in, arrived, mesh_other, weight_own, weight_out, weight_other, pooled, pooled_other,
    hidden, hidden_other, inner, total, stage,
    link_send, link_recv, sum_send, sum_recv, back_send, back_recv, mp_send, mp_recv,
):
    bands = sums_ref.shape[0]
    blocks, edge, half = mesh_ref.shape
    part = edge // chunks
    flat = (blocks * part, half)

    def rows_of(chunk):
        return pl.ds(chunk * part, part)

    def hop_at(turn):
        return 1 + lax.rem(turn + bands // 2 - 1, bands - 1)
    me = lax.axis_index("band")
    core = lax.axis_index("mp")
    peer = 1 - core
    across = {"mp": peer}
    mine = pl.multiple_of(core * half, half)
    theirs = pl.multiple_of(peer * half, half)

    barrier = pltpu.get_barrier_semaphore()

    def greet(hop, carry):
        pl.semaphore_signal(
            barrier,
            inc=1,
            device_id={"band": lax.rem(me + hop, bands)},
            device_id_type=pl.DeviceIdType.MESH,
        )
        return carry

    lax.fori_loop(1, bands, greet, 0)
    pl.semaphore_signal(barrier, inc=1, device_id=across, device_id_type=pl.DeviceIdType.MESH)

    def spread(patch, carry):
        link_out[patch] = jnp.full(link_out.shape[1:], linked_ref[0, patch], jnp.int32)
        return carry

    lax.fori_loop(0, bands, spread, 0)
    pl.semaphore_wait(barrier, bands)

    def link_copy(patch):
        return push(
            link_out.at[patch], link_in.at[me], link_send.at[patch], link_recv.at[me],
            {"band": patch},
        )

    def sum_copy(chunk, patch, sender):
        return push(
            sums_ref.at[patch, rows_of(chunk)],
            arrived.at[sender, rows_of(chunk)],
            sum_send.at[chunk, patch],
            sum_recv.at[chunk, sender],
            {"band": patch},
        )

    def back_copy(chunk, band, sender):
        return push(
            stage.at[band, rows_of(chunk)],
            returned_ref.at[sender, rows_of(chunk)],
            back_send.at[chunk, band],
            back_recv.at[chunk, sender],
            {"band": band},
        )

    def send_links(hop, carry):
        link_copy(lax.rem(me + hop, bands)).start()
        return carry

    lax.fori_loop(1, bands, send_links, 0)
    for chunk in range(chunks):

        def send_sums(turn, carry, chunk=chunk):
            sum_copy(chunk, lax.rem(me + hop_at(turn), bands), me).start()
            return carry

        lax.fori_loop(0, bands - 1, send_sums, 0)

    mesh_copy = push(mesh_ref, mesh_other, mp_send.at[0], mp_recv.at[0], across)
    mesh_copy.start()
    weight_copies = [
        push(
            weight_out.at[which],
            weight_other.at[which],
            mp_send.at[1 + which],
            mp_recv.at[1 + which],
            across,
        )
        for which in range(2)
    ]
    for which in range(2):
        plane = out_weight_ref[:, which, :]
        swap = core == 0
        weight_own[which] = jnp.where(swap, plane[:, :half], plane[:, half:])
        weight_out[which] = jnp.where(swap, plane[:, half:], plane[:, :half])
        weight_copies[which].start()

    inner[...] = matmul(
        mesh_ref[...].reshape(blocks * edge, half), self_ref[pl.ds(mine, half), :]
    ).reshape(inner.shape)
    mesh_copy.wait()
    inner[...] += matmul(
        mesh_other[...].reshape(blocks * edge, half), self_ref[pl.ds(theirs, half), :]
    ).reshape(inner.shape)
    for copy in weight_copies:
        copy.wait()
    own_link = link_out[me, 0:1, :]

    for chunk in range(chunks):
        rows = rows_of(chunk)
        own = sums_ref[me, rows, :].astype(jnp.float32)
        for block in range(blocks):
            total[block] = jnp.where(own_link == block, own, 0.0)

        def gather(turn, carry, chunk=chunk, rows=rows):
            band = lax.rem(me + bands - hop_at(turn), bands)
            if chunk == 0:
                push(
                    link_out.at[band], link_in.at[band], link_send.at[band],
                    link_recv.at[band], {"band": band},
                ).wait_recv()
            sum_copy(chunk, band, band).wait_recv()
            value = arrived[band, rows, :].astype(jnp.float32)
            link = link_in[band, 0:1, :]
            for block in range(blocks):
                total[block] += jnp.where(link == block, value, 0.0)
            return carry

        lax.fori_loop(0, bands - 1, gather, 0)

        pooled[chunk] = total[...].reshape(flat).astype(pooled.dtype)
        pooled_copy = push(
            pooled.at[chunk], pooled_other.at[chunk],
            mp_send.at[3 + chunk], mp_recv.at[3 + chunk], across,
        )
        pooled_copy.start()
        before = inner[:, rows, :].reshape(flat) + matmul(
            pooled[chunk], pooled_weight_ref[pl.ds(mine, half), :]
        )
        pooled_copy.wait()
        before += matmul(pooled_other[chunk], pooled_weight_ref[pl.ds(theirs, half), :])
        hidden[chunk] = silu(before).astype(hidden.dtype)
        hidden_copy = push(
            hidden.at[chunk], hidden_other.at[chunk],
            mp_send.at[3 + chunks + chunk], mp_recv.at[3 + chunks + chunk], across,
        )
        hidden_copy.start()
        source = matmul(hidden[chunk], weight_own[1])
        residual = matmul(hidden[chunk], weight_own[0])
        hidden_copy.wait()
        source += matmul(hidden_other[chunk], weight_other[1])
        total[...] = source.astype(jnp.bfloat16).astype(jnp.float32).reshape(total.shape)

        def picked(link):
            value = total[0]
            for block in range(1, blocks):
                value = jnp.where(link == block, total[block], value)
            return value.astype(stage.dtype)

        def send_back(turn, carry, chunk=chunk, rows=rows, picked=picked):
            band = lax.rem(me + hop_at(turn), bands)
            stage[band, rows, :] = picked(link_in[band, 0:1, :])
            back_copy(chunk, band, me).start()
            return carry

        lax.fori_loop(0, bands - 1, send_back, 0)
        returned_ref[me, rows, :] = picked(own_link)
        residual += matmul(hidden_other[chunk], weight_other[0])
        state_ref[:, rows, :] = (
            mesh_ref[:, rows, :].astype(jnp.float32) + residual.reshape(total.shape)
        ).astype(state_ref.dtype)

    def finish(turn, carry):
        band = lax.rem(me + bands - hop_at(turn), bands)
        link_copy(band).wait_send()
        for chunk in range(chunks):
            back_copy(chunk, band, band).wait_recv()
            sum_copy(chunk, band, me).wait_send()
            back_copy(chunk, band, me).wait_send()
        return carry

    lax.fori_loop(0, bands - 1, finish, 0)


def update_nodes(sums, linked, mesh_nodes, self_weight, pooled_weight, out_weight):
    bands, edge, half = sums.shape
    mesh_blocks = mesh_nodes.reshape(-1, edge, half)
    blocks = mesh_blocks.shape[0]
    chunks = 2
    nodes = VMEM((chunks, blocks * edge // chunks, half), jnp.bfloat16)
    by_band = pltpu.SemaphoreType.DMA((bands,))
    by_part = pltpu.SemaphoreType.DMA((chunks, bands))
    by_use = pltpu.SemaphoreType.DMA((3 + 2 * chunks,))
    vmem = pl.BlockSpec(memory_space=VMEM)
    state, returned = pl.pallas_call(
        functools.partial(node_kernel, chunks),
        out_shape=(
            jax.ShapeDtypeStruct(mesh_blocks.shape, jnp.bfloat16),
            jax.ShapeDtypeStruct(sums.shape, jnp.bfloat16),
        ),
        in_specs=[vmem, pl.BlockSpec(memory_space=pltpu.SMEM)] + [vmem] * 4,
        out_specs=(vmem, vmem),
        scratch_shapes=[
            VMEM((bands, 8, half), jnp.int32),
            VMEM((bands, 8, half), jnp.int32),
            VMEM(sums.shape, jnp.bfloat16),
            VMEM(mesh_blocks.shape, jnp.bfloat16),
            VMEM((2, out_weight.shape[0], half), jnp.bfloat16),
            VMEM((2, out_weight.shape[0], half), jnp.bfloat16),
            VMEM((2, out_weight.shape[0], half), jnp.bfloat16),
            nodes,
            nodes,
            nodes,
            nodes,
            VMEM(mesh_blocks.shape, jnp.float32),
            VMEM((blocks, edge // chunks, half), jnp.float32),
            VMEM(sums.shape, jnp.bfloat16),
        ]
        + [by_band] * 2
        + [by_part] * 4
        + [by_use] * 2,
        compiler_params=pltpu.CompilerParams(
            collective_id=1, has_side_effects=True, vmem_limit_bytes=VMEM_LIMIT
        ),
        name="update_nodes",
    )(sums, linked, mesh_blocks, self_weight, pooled_weight, out_weight)
    return state.reshape(mesh_nodes.shape), returned


def per_device(
    grid_nodes,
    mesh_nodes,
    send_weight,
    self_weight,
    pooled_weight,
    out_weight,
    encode_source,
    encode_slot,
    encode_tiles,
    slot_block,
    decode_slot,
    decode_target,
    decode_tiles,
):
    band_count = lax.axis_size("band")
    tile_edge = encode_tiles.shape[1]
    feature_width = grid_nodes.shape[1]
    grid_blocks = grid_nodes.shape[0] // tile_edge
    message = messages(grid_nodes, send_weight)
    message_blocks = message.reshape(grid_blocks, tile_edge, feature_width)
    slot_sums = encode(message_blocks, encode_tiles, encode_source, encode_slot, band_count)
    mesh_state, returned = update_nodes(
        slot_sums, slot_block, mesh_nodes, self_weight, pooled_weight, out_weight
    )
    grid_state = decode(
        grid_nodes.reshape(grid_blocks, tile_edge, feature_width),
        returned,
        decode_tiles,
        decode_slot,
        decode_target,
    ).reshape(grid_nodes.shape)
    return (grid_state, mesh_state)


def solution(mesh):
    return jax.shard_map(
        per_device,
        mesh=mesh,
        in_specs=(
            P("band", "mp"),
            P("band", "mp"),
            P(None, "mp"),
            P(None, "mp"),
            P(None, "mp"),
            P("mp", None, None),
            P("band"),
            P("band"),
            P("band", None, None),
            P("band", None),
            P("band"),
            P("band"),
            P("band", None, None),
        ),
        out_specs=(P("band", "mp"), P("band", "mp")),
        check_vma=False,
    )
```

```python
import functools

import jax
import jax.numpy as jnp
from jax import lax
from jax.experimental import pallas as pl
from jax.experimental.pallas import tpu as pltpu
from jax.sharding import PartitionSpec as P

VMEM = pltpu.VMEM
VMEM_LIMIT = 56 * 1024 * 1024


def divisor_at_most(count, most):
    return max(part for part in range(1, most + 1) if count % part == 0)


def tile_sums(group, tile_at, rows_ref, tiles_ref, into_ref, from_ref, totals):
    for local in range(group):
        place = tile_at + local
        product = jnp.dot(
            tiles_ref[local], rows_ref[from_ref[place]], preferred_element_type=jnp.float32
        )
        totals[local % len(totals)][into_ref[place]] += product


def encode_kernel(group, source_ref, slot_ref, message_ref, tiles_ref, out_ref, *totals):
    step = pl.program_id(0)

    @pl.when(step == 0)
    def _():
        for total in totals:
            total[...] = jnp.zeros_like(total)

    tile_sums(group, step * group, message_ref, tiles_ref, slot_ref, source_ref, totals)

    @pl.when(step == pl.num_programs(0) - 1)
    def _():
        out_ref[...] = sum(total[...] for total in totals).astype(out_ref.dtype)


def decode_kernel(
    group, slot_ref, target_ref, grid_hbm, rows_ref, tiles_ref, out_ref, grid_ref, load_sem, *totals
):
    step = pl.program_id(0)
    load = pltpu.make_async_copy(grid_hbm, grid_ref, load_sem)

    @pl.when(step == 0)
    def _():
        load.start()
        for total in totals:
            total[...] = jnp.zeros_like(total)

    tile_sums(group, step * group, rows_ref, tiles_ref, target_ref, slot_ref, totals)

    @pl.when(step == pl.num_programs(0) - 1)
    def _():
        load.wait()
        summed = sum(total[...] for total in totals)
        out_ref[...] = (grid_ref[...].astype(jnp.float32) + summed).astype(out_ref.dtype)


def whole(array):
    return pl.BlockSpec(array.shape, lambda step, *_: (0,) * array.ndim)


def encode(message_blocks, tiles, source, slot, slots):
    count, edge, _ = tiles.shape
    width = message_blocks.shape[2]
    group = divisor_at_most(count, 96)
    out = jax.ShapeDtypeStruct((slots, edge, width), jnp.bfloat16)
    return pl.pallas_call(
        functools.partial(encode_kernel, group),
        out_shape=out,
        grid_spec=pltpu.PrefetchScalarGridSpec(
            num_scalar_prefetch=2,
            grid=(count // group,),
            in_specs=[
                whole(message_blocks),
                pl.BlockSpec((group, edge, edge), lambda step, *_: (step, 0, 0)),
            ],
            out_specs=whole(out),
            scratch_shapes=[VMEM((slots, edge, width), jnp.float32)] * 1,
        ),
        compiler_params=pltpu.CompilerParams(vmem_limit_bytes=VMEM_LIMIT),
        name="encode",
    )(source, slot, message_blocks, tiles)


def decode(grid_blocks, rows, tiles, slot, target):
    count, edge, _ = tiles.shape
    group = divisor_at_most(count, 96)
    return pl.pallas_call(
        functools.partial(decode_kernel, group),
        out_shape=jax.ShapeDtypeStruct(grid_blocks.shape, jnp.bfloat16),
        grid_spec=pltpu.PrefetchScalarGridSpec(
            num_scalar_prefetch=2,
            grid=(count // group,),
            in_specs=[
                pl.BlockSpec(memory_space=pl.ANY),
                whole(rows),
                pl.BlockSpec((group, edge, edge), lambda step, *_: (step, 0, 0)),
            ],
            out_specs=whole(grid_blocks),
            scratch_shapes=[VMEM(grid_blocks.shape, jnp.bfloat16), pltpu.SemaphoreType.DMA]
            + [VMEM(grid_blocks.shape, jnp.float32)] * 1,
        ),
        compiler_params=pltpu.CompilerParams(vmem_limit_bytes=VMEM_LIMIT),
        name="decode",
    )(slot, target, grid_blocks, rows, tiles)


def silu(value):
    return value / (1.0 + jnp.exp(-value))


def push(source, target, send_sem, recv_sem, device):
    return pltpu.make_async_remote_copy(
        src_ref=source,
        dst_ref=target,
        send_sem=send_sem,
        recv_sem=recv_sem,
        device_id=device,
        device_id_type=pl.DeviceIdType.MESH,
    )


def matmul(left, right):
    return jnp.dot(left, right, preferred_element_type=jnp.float32)


def message_kernel(parts, grid_hbm, weight_ref, out_ref, own, other, load_sem, send_sem, recv_sem):
    me = lax.axis_index("mp")
    peer = 1 - me
    rows = own.shape[0] // parts
    half = own.shape[1]

    def part(ref, at):
        return ref.at[pl.ds(at * rows, rows)]

    loads = [
        pltpu.make_async_copy(part(grid_hbm, at), part(own, at), load_sem.at[at])
        for at in range(parts)
    ]
    for load in loads:
        load.start()
    barrier = pltpu.get_barrier_semaphore()
    pl.semaphore_signal(
        barrier, inc=1, device_id={"mp": peer}, device_id_type=pl.DeviceIdType.MESH
    )
    pl.semaphore_wait(barrier, 1)
    sends = [
        push(part(grid_hbm, at), part(other, at), send_sem.at[at], recv_sem.at[at], {"mp": peer})
        for at in range(parts)
    ]
    for send in sends:
        send.start()
    own_weight = weight_ref[pl.ds(pl.multiple_of(me * half, half), half), :]
    other_weight = weight_ref[pl.ds(pl.multiple_of(peer * half, half), half), :]
    for at in range(parts):
        loads[at].wait()
        sends[at].wait_recv()
        span = pl.ds(at * rows, rows)
        total = matmul(own[span, :], own_weight) + matmul(other[span, :], other_weight)
        out_ref[span, :] = silu(total).astype(out_ref.dtype)
    for send in sends:
        send.wait_send()


def messages(grid_nodes, send_weight):
    rows, half = grid_nodes.shape
    parts = 4
    return pl.pallas_call(
        functools.partial(message_kernel, parts),
        out_shape=jax.ShapeDtypeStruct((rows, send_weight.shape[1]), jnp.bfloat16),
        in_specs=[pl.BlockSpec(memory_space=pl.ANY), pl.BlockSpec(memory_space=VMEM)],
        out_specs=pl.BlockSpec(memory_space=VMEM),
        scratch_shapes=[VMEM((rows, half), jnp.bfloat16)] * 2
        + [pltpu.SemaphoreType.DMA((parts,))] * 3,
        compiler_params=pltpu.CompilerParams(
            collective_id=0, has_side_effects=True, vmem_limit_bytes=VMEM_LIMIT
        ),
        name="messages",
    )(grid_nodes, send_weight)


def node_kernel(
    chunks, sums_ref, linked_ref, mesh_ref, self_ref, pooled_weight_ref, out_weight_ref,
    state_ref, returned_ref,
    link_out, link_in, arrived, mesh_other, weight_own, weight_out, weight_other, pooled, pooled_other,
    hidden, hidden_other, inner, total, stage,
    link_send, link_recv, sum_send, sum_recv, back_send, back_recv, mp_send, mp_recv,
):
    bands = sums_ref.shape[0]
    blocks, edge, half = mesh_ref.shape
    part = edge // chunks
    flat = (blocks * part, half)

    def rows_of(chunk):
        return pl.ds(chunk * part, part)

    def hop_at(turn):
        return 1 + turn
    me = lax.axis_index("band")
    core = lax.axis_index("mp")
    peer = 1 - core
    across = {"mp": peer}
    mine = pl.multiple_of(core * half, half)
    theirs = pl.multiple_of(peer * half, half)

    barrier = pltpu.get_barrier_semaphore()

    def greet(hop, carry):
        pl.semaphore_signal(
            barrier,
            inc=1,
            device_id={"band": lax.rem(me + hop, bands)},
            device_id_type=pl.DeviceIdType.MESH,
        )
        return carry

    lax.fori_loop(1, bands, greet, 0)
    pl.semaphore_signal(barrier, inc=1, device_id=across, device_id_type=pl.DeviceIdType.MESH)

    def spread(patch, carry):
        link_out[patch] = jnp.full(link_out.shape[1:], linked_ref[0, patch], jnp.int32)
        return carry

    lax.fori_loop(0, bands, spread, 0)
    pl.semaphore_wait(barrier, bands)

    def link_copy(patch):
        return push(
            link_out.at[patch], link_in.at[me], link_send.at[patch], link_recv.at[me],
            {"band": patch},
        )

    def sum_copy(chunk, patch, sender):
        return push(
            sums_ref.at[patch, rows_of(chunk)],
            arrived.at[sender, rows_of(chunk)],
            sum_send.at[chunk, patch],
            sum_recv.at[chunk, sender],
            {"band": patch},
        )

    def back_copy(chunk, band, sender):
        return push(
            stage.at[band, rows_of(chunk)],
            returned_ref.at[sender, rows_of(chunk)],
            back_send.at[chunk, band],
            back_recv.at[chunk, sender],
            {"band": band},
        )

    def send_links(hop, carry):
        link_copy(lax.rem(me + hop, bands)).start()
        return carry

    lax.fori_loop(1, bands, send_links, 0)
    for chunk in range(chunks):

        def send_sums(turn, carry, chunk=chunk):
            sum_copy(chunk, lax.rem(me + hop_at(turn), bands), me).start()
            return carry

        lax.fori_loop(0, bands - 1, send_sums, 0)

    mesh_copy = push(mesh_ref, mesh_other, mp_send.at[0], mp_recv.at[0], across)
    mesh_copy.start()
    weight_copies = [
        push(
            weight_out.at[which],
            weight_other.at[which],
            mp_send.at[1 + which],
            mp_recv.at[1 + which],
            across,
        )
        for which in range(2)
    ]
    for which in range(2):
        plane = out_weight_ref[:, which, :]
        swap = core == 0
        weight_own[which] = jnp.where(swap, plane[:, :half], plane[:, half:])
        weight_out[which] = jnp.where(swap, plane[:, half:], plane[:, :half])
        weight_copies[which].start()

    inner[...] = matmul(
        mesh_ref[...].reshape(blocks * edge, half), self_ref[pl.ds(mine, half), :]
    ).reshape(inner.shape)
    mesh_copy.wait()
    inner[...] += matmul(
        mesh_other[...].reshape(blocks * edge, half), self_ref[pl.ds(theirs, half), :]
    ).reshape(inner.shape)
    for copy in weight_copies:
        copy.wait()
    own_link = link_out[me, 0:1, :]

    for chunk in range(chunks):
        rows = rows_of(chunk)
        own = sums_ref[me, rows, :].astype(jnp.float32)
        for block in range(blocks):
            total[block] = jnp.where(own_link == block, own, 0.0)

        def gather(turn, carry, chunk=chunk, rows=rows):
            band = lax.rem(me + bands - hop_at(turn), bands)
            if chunk == 0:
                push(
                    link_out.at[band], link_in.at[band], link_send.at[band],
                    link_recv.at[band], {"band": band},
                ).wait_recv()
            sum_copy(chunk, band, band).wait_recv()
            value = arrived[band, rows, :].astype(jnp.float32)
            link = link_in[band, 0:1, :]
            for block in range(blocks):
                total[block] += jnp.where(link == block, value, 0.0)
            return carry

        lax.fori_loop(0, bands - 1, gather, 0)

        pooled[chunk] = total[...].reshape(flat).astype(pooled.dtype)
        pooled_copy = push(
            pooled.at[chunk], pooled_other.at[chunk],
            mp_send.at[3 + chunk], mp_recv.at[3 + chunk], across,
        )
        pooled_copy.start()
        before = inner[:, rows, :].reshape(flat) + matmul(
            pooled[chunk], pooled_weight_ref[pl.ds(mine, half), :]
        )
        pooled_copy.wait()
        before += matmul(pooled_other[chunk], pooled_weight_ref[pl.ds(theirs, half), :])
        hidden[chunk] = silu(before).astype(hidden.dtype)
        hidden_copy = push(
            hidden.at[chunk], hidden_other.at[chunk],
            mp_send.at[3 + chunks + chunk], mp_recv.at[3 + chunks + chunk], across,
        )
        hidden_copy.start()
        source = matmul(hidden[chunk], weight_own[1])
        residual = matmul(hidden[chunk], weight_own[0])
        hidden_copy.wait()
        source += matmul(hidden_other[chunk], weight_other[1])
        total[...] = source.astype(jnp.bfloat16).astype(jnp.float32).reshape(total.shape)

        def picked(link):
            value = total[0]
            for block in range(1, blocks):
                value = jnp.where(link == block, total[block], value)
            return value.astype(stage.dtype)

        def send_back(turn, carry, chunk=chunk, rows=rows, picked=picked):
            band = lax.rem(me + hop_at(turn), bands)
            stage[band, rows, :] = picked(link_in[band, 0:1, :])
            back_copy(chunk, band, me).start()
            return carry

        lax.fori_loop(0, bands - 1, send_back, 0)
        returned_ref[me, rows, :] = picked(own_link)
        residual += matmul(hidden_other[chunk], weight_other[0])
        state_ref[:, rows, :] = (
            mesh_ref[:, rows, :].astype(jnp.float32) + residual.reshape(total.shape)
        ).astype(state_ref.dtype)

    def finish(turn, carry):
        band = lax.rem(me + bands - hop_at(turn), bands)
        link_copy(band).wait_send()
        for chunk in range(chunks):
            back_copy(chunk, band, band).wait_recv()
            sum_copy(chunk, band, me).wait_send()
            back_copy(chunk, band, me).wait_send()
        return carry

    lax.fori_loop(0, bands - 1, finish, 0)


def update_nodes(sums, linked, mesh_nodes, self_weight, pooled_weight, out_weight):
    bands, edge, half = sums.shape
    mesh_blocks = mesh_nodes.reshape(-1, edge, half)
    blocks = mesh_blocks.shape[0]
    chunks = 2
    nodes = VMEM((chunks, blocks * edge // chunks, half), jnp.bfloat16)
    by_band = pltpu.SemaphoreType.DMA((bands,))
    by_part = pltpu.SemaphoreType.DMA((chunks, bands))
    by_use = pltpu.SemaphoreType.DMA((3 + 2 * chunks,))
    vmem = pl.BlockSpec(memory_space=VMEM)
    state, returned = pl.pallas_call(
        functools.partial(node_kernel, chunks),
        out_shape=(
            jax.ShapeDtypeStruct(mesh_blocks.shape, jnp.bfloat16),
            jax.ShapeDtypeStruct(sums.shape, jnp.bfloat16),
        ),
        in_specs=[vmem, pl.BlockSpec(memory_space=pltpu.SMEM)] + [vmem] * 4,
        out_specs=(vmem, vmem),
        scratch_shapes=[
            VMEM((bands, 8, half), jnp.int32),
            VMEM((bands, 8, half), jnp.int32),
            VMEM(sums.shape, jnp.bfloat16),
            VMEM(mesh_blocks.shape, jnp.bfloat16),
            VMEM((2, out_weight.shape[0], half), jnp.bfloat16),
            VMEM((2, out_weight.shape[0], half), jnp.bfloat16),
            VMEM((2, out_weight.shape[0], half), jnp.bfloat16),
            nodes,
            nodes,
            nodes,
            nodes,
            VMEM(mesh_blocks.shape, jnp.float32),
            VMEM((blocks, edge // chunks, half), jnp.float32),
            VMEM(sums.shape, jnp.bfloat16),
        ]
        + [by_band] * 2
        + [by_part] * 4
        + [by_use] * 2,
        compiler_params=pltpu.CompilerParams(
            collective_id=1, has_side_effects=True, vmem_limit_bytes=VMEM_LIMIT
        ),
        name="update_nodes",
    )(sums, linked, mesh_blocks, self_weight, pooled_weight, out_weight)
    return state.reshape(mesh_nodes.shape), returned


def per_device(
    grid_nodes,
    mesh_nodes,
    send_weight,
    self_weight,
    pooled_weight,
    out_weight,
    encode_source,
    encode_slot,
    encode_tiles,
    slot_block,
    decode_slot,
    decode_target,
    decode_tiles,
):
    band_count = lax.axis_size("band")
    tile_edge = encode_tiles.shape[1]
    feature_width = grid_nodes.shape[1]
    grid_blocks = grid_nodes.shape[0] // tile_edge
    message = messages(grid_nodes, send_weight)
    message_blocks = message.reshape(grid_blocks, tile_edge, feature_width)
    slot_sums = encode(message_blocks, encode_tiles, encode_source, encode_slot, band_count)
    mesh_state, returned = update_nodes(
        slot_sums, slot_block, mesh_nodes, self_weight, pooled_weight, out_weight
    )
    grid_state = decode(
        grid_nodes.reshape(grid_blocks, tile_edge, feature_width),
        returned,
        decode_tiles,
        decode_slot,
        decode_target,
    ).reshape(grid_nodes.shape)
    return (grid_state, mesh_state)


def solution(mesh):
    return jax.shard_map(
        per_device,
        mesh=mesh,
        in_specs=(
            P("band", "mp"),
            P("band", "mp"),
            P(None, "mp"),
            P(None, "mp"),
            P(None, "mp"),
            P("mp", None, None),
            P("band"),
            P("band"),
            P("band", None, None),
            P("band", None),
            P("band"),
            P("band"),
            P("band", None, None),
        ),
        out_specs=(P("band", "mp"), P("band", "mp")),
        check_vma=False,
    )
```
